32 devices in a mesh: groups: 2 (over x), tensor: 8 (over z, y), seq: 2 (over core).
Axes of the slice: x: 2, y: 2, z: 4, core: 2. Of those that a mesh axis runs over, the one named last changes fastest.
Arguments:
- queries: bfloat16 [64, 64, 128], P('groups'), parts along dimension 0
- keys: bfloat16 [32768, 64, 128], P(('tensor', 'seq'), 'groups'), parts along dimension 1
- values: bfloat16 [32768, 64, 128], P(('tensor', 'seq'), 'groups'), parts along dimension 1, may hold values from -6 to 6
- lengths: int32 [64], P('groups'), parts along dimension 0, may hold values from 2 to 4096, as said below
- out_weight: bfloat16 [8192, 8192], P(('tensor', 'seq')), may hold values from -0.75 to 0.75
Outputs:
- mixed: bfloat16 [64, 8192], P('groups', ('tensor', 'seq')), parts along dimension 0
The draws below stay inside these ranges and needn't reach their ends.
There are 2 independent parts, one for each index of `groups`. The reference program is written for one: setup_inputs(seed, part) draws one part's arguments, and reference() takes and returns one part's arrays. A program takes and returns all parts, laid end to end along the dimension named above; an argument that names none is the same for every part. Nothing has to cross between parts.
Inputs may be any that keep to these rules, and one draw needn't show every extreme that they name: `lengths`: every length is at least 2, and in each part one sequence has exactly 4096 live slots.
All inputs are finite; a program needn't handle non-finite values.
Results may differ from the reference program's by a relative error of at most 0.005.
Values sent between devices are 32-bit elements; how exact they have to be, the bound alone decides.
A program may use at most 128 MiB of HBM per device.

```python
import jax
import jax.numpy as jnp
from jax import lax

D = 8192
HQ = 64
KVH = 8
HD = 128
BATCH = 32
CACHE = 4096


def draw_queries(key, part):
    base = 1.5 * jax.random.normal(jax.random.fold_in(key, 11), (BATCH, HQ, HD), jnp.float32)
    return base.astype(jnp.bfloat16)


def draw_keys(key, part):
    base = jax.random.normal(jax.random.fold_in(key, 22), (KVH * CACHE, BATCH, HD), jnp.float32)
    return base.astype(jnp.bfloat16)


def draw_lengths(key, part):
    spread = jax.random.randint(jax.random.fold_in(key, 31), (BATCH,), 2, CACHE + 1)
    chosen = jax.random.randint(jax.random.fold_in(key, 32), (), 0, BATCH)
    return jnp.where(jnp.arange(BATCH) == chosen, CACHE, spread).astype(jnp.int32)


def raised(result, stream_key, source, target, parts, factor):
    owner, partner = [(jnp.arange(result.shape[axis_at]) // (result.shape[axis_at] // parts)).reshape([-1 if axis == axis_at else 1 for axis in range(result.ndim)]) for axis_at in (source, target)]
    chosen = jax.random.permutation(stream_key, parts)[partner]
    strong = (owner == chosen) | (owner == (partner + parts // 2) % parts)
    return jnp.where(strong, factor * result, result)


def block_scale(key, dims, cuts, least, high):
    loudness, own = 1.0, jax.random.fold_in(key, 6)
    for axis_at, shards_of in cuts:
        draws = jnp.exp(jax.random.uniform(jax.random.fold_in(own, axis_at), (shards_of,), jnp.float32, least / len(cuts), high / len(cuts)))
        loudness = loudness * jnp.repeat(draws, dims[axis_at] // shards_of).reshape([-1 if axis == axis_at else 1 for axis in range(len(dims))])
    return loudness


def scatter_about(own_key, shape, scale, most, pieces=(), kind=jnp.bfloat16):
    entries = scale * jax.random.normal(own_key, shape, jnp.float32)
    if pieces:
        entries = entries * block_scale(own_key, shape, pieces, -0.22, 0.18)
    return jnp.clip(entries, -most, most).astype(kind)


def heavy_noise(rng, shape, scale, most, cuts, heavy, held_as=jnp.bfloat16):
    result = scale * jax.random.normal(rng, shape, jnp.float32)
    if cuts:
        result = result * block_scale(rng, shape, cuts, -0.22, 0.18)
    return jnp.clip(raised(result, jax.random.fold_in(rng, 3), *heavy), -most, most).astype(held_as)


def setup_inputs(seed: int = 0, part: int = 0) -> dict:
    arg_keys = jax.random.split(jax.random.key(seed), 6)
    part_keys = jax.random.split(jax.random.fold_in(arg_keys[5], part), 6)
    queries = draw_queries(jax.random.fold_in(jax.random.fold_in(arg_keys[5], part), 71), part)
    keys = draw_keys(jax.random.fold_in(jax.random.fold_in(arg_keys[5], part), 71), part)
    values = scatter_about(part_keys[2], (KVH * CACHE, BATCH, HD), 1.0, 6.0, ((0, 16),))
    lengths = draw_lengths(jax.random.fold_in(jax.random.fold_in(arg_keys[5], part), 71), part)
    out_weight = heavy_noise(arg_keys[4], (HQ * HD, D), HD ** -0.5, 0.75, ((0, 16),), (0, 1, 16, 2.0))
    return {"queries": queries, "keys": keys, "values": values, "lengths": lengths, "out_weight": out_weight}


masked_fill = -1e+30

def reference(queries, keys, values, lengths, out_weight):
    per_group = HQ // KVH
    positions = jnp.arange(CACHE, dtype=jnp.int32)
    live = (positions[None, :] < lengths[:, None])[:, None, :]
    results = []
    for head in range(KVH):
        head_keys = keys[head * CACHE:(head + 1) * CACHE].astype(jnp.float32)
        head_values = values[head * CACHE:(head + 1) * CACHE].astype(jnp.float32)
        head_queries = queries[:, head * per_group:(head + 1) * per_group].astype(jnp.float32)
        scores = jnp.einsum('bgd,pbd->bgp', head_queries, head_keys, precision=lax.Precision.HIGHEST) / jnp.sqrt(jnp.float32(HD))
        scores = jnp.where(live, scores, masked_fill)
        highest = lax.optimization_barrier(jnp.max(scores, axis=2))
        weights = jnp.where(live, jnp.exp(scores - highest[..., None]), 0.0)
        totals = lax.optimization_barrier(jnp.sum(weights, axis=2))
        accum = jnp.einsum('bgp,pbd->bgd', weights, head_values, precision=lax.Precision.HIGHEST)
        results.append(accum / totals[..., None])
    attended = jnp.concatenate(results, axis=1).reshape(BATCH, HQ * HD).astype(jnp.bfloat16)
    return jnp.dot(attended, out_weight, preferred_element_type=jnp.float32).astype(jnp.bfloat16)
```

```python
import functools
import math

import jax
import jax.numpy as jnp
from jax import lax
from jax.experimental import pallas as pl
from jax.experimental.pallas import tpu as pltpu
from jax.sharding import PartitionSpec as P

HQ = 64
KVH = 8
CACHE = 4096

MESH = pl.DeviceIdType.MESH
masked_fill = -1e30
ROWS = 16
STEP = 64


def kernel(
    n_tensor, n_seq, lengths, queries, keys, values, weight, out,
    kbuf, vbuf, wbuf, qbuf, qflat, qdiag, scores, acc, stats, got, flat_att,
    part, from_core, pair, from_near, line, from_far,
    k_sem, v_sem, w_sem, q_sem, stat_sems, core_sems, near_sems, far_sems,
):
    n_flat = n_tensor * n_seq
    span, batch, head_size = keys.shape
    per_group = HQ // KVH
    n_split = CACHE // span
    groups = batch // ROWS
    lanes = ROWS * per_group
    wide = groups * lanes
    depth = groups * head_size
    heads_own = HQ // n_flat
    n_chunks = span // STEP
    cols = out.shape[1]
    n_far = n_tensor // 2
    wide_cols = 2 * n_seq * cols

    group = lax.axis_index("groups")
    tensor = lax.axis_index("tensor")
    core = lax.axis_index("seq")
    flat = tensor * n_seq + core
    kv_head = flat // n_split
    place = flat % n_split
    far, near = tensor // 2, tensor % 2
    other_core = 1 - core

    offsets = sorted(range(n_far), key=lambda off: (-min(off, n_far - off), off))

    def member(index):
        return (group, index // n_seq, index % n_seq)

    stat_peers = [member(kv_head * n_split + (place + k) % n_split) for k in range(1, n_split)]
    core_peer = (group, tensor, other_core)
    near_peer = (group, far * 2 + 1 - near, core)
    far_peers = [(group, (far + off) % n_far * 2 + near, core) for off in offsets]

    barrier = pltpu.get_barrier_semaphore()
    greeted = stat_peers + [core_peer, near_peer] + [
        peer for off, peer in zip(offsets, far_peers) if off
    ]
    for peer in greeted:
        pl.semaphore_signal(barrier, inc=1, device_id=peer, device_id_type=MESH)

    q_rows = ROWS if per_group < ROWS else per_group
    q_start = pl.multiple_of(kv_head * per_group // q_rows * q_rows, q_rows)
    q_copy = pltpu.make_async_copy(queries.at[:, pl.ds(q_start, q_rows), :], qbuf, q_sem)
    q_copy.start()

    def k_copy(c):
        piece = pl.ds(c * STEP, STEP)
        return pltpu.make_async_copy(keys.at[piece], kbuf.at[piece], k_sem.at[c])

    def v_copy(c):
        piece = pl.ds(c * STEP, STEP)
        return pltpu.make_async_copy(values.at[piece], vbuf.at[piece], v_sem.at[c])

    def w_copy(k):
        start = pl.multiple_of((far + offsets[k]) % n_far * wide_cols, wide_cols)
        return pltpu.make_async_copy(weight.at[:, pl.ds(start, wide_cols)], wbuf.at[k], w_sem.at[k])

    @pl.loop(0, n_chunks)
    def _(c):
        k_copy(c).start()

    @pl.loop(0, n_chunks)
    def _(c):
        v_copy(c).start()

    for k in range(n_far):
        w_copy(k).start()

    lane = lax.broadcasted_iota(jnp.int32, (8, wide), 1)
    sub = lax.broadcasted_iota(jnp.int32, (8, wide), 0)
    home = lane % 8
    low = lane % ROWS < 8
    turn = (sub - home + 8) % 8
    at_home = sub == home
    sequence = lane // lanes * ROWS + lane % ROWS
    live_slots = jnp.zeros((8, wide), jnp.int32)
    for b in range(batch):
        live_slots = jnp.where(sequence == b, lengths[b], live_slots)
    first_slot = place * span
    room = live_slots - first_slot - turn

    q_copy.wait()
    q = qbuf[...].astype(jnp.float32)
    if q_rows > per_group:
        q = jnp.where(kv_head % 2 == 0, q[:, :per_group], q[:, per_group:])
    qflat[...] = q
    zero = jnp.zeros((head_size, lanes), jnp.bfloat16)
    for g in range(groups):
        block = jnp.concatenate(
            [qflat[g * ROWS:(g + 1) * ROWS, j, :] for j in range(per_group)], axis=0
        )
        for h in range(groups):
            qdiag[g * head_size:(g + 1) * head_size, h * lanes:(h + 1) * lanes] = (
                block.T.astype(jnp.bfloat16) if g == h else zero
            )

    def side_by_side(buf, c):
        piece = buf[pl.ds(c * STEP, STEP)]
        return jnp.concatenate(
            [
                piece[:, g * ROWS:(g + 1) * ROWS].reshape(STEP * ROWS, head_size)
                for g in range(groups)
            ],
            axis=1,
        )

    blocks = STEP // 8

    def base_of(c):
        return c * STEP + 8 * lax.broadcasted_iota(jnp.int32, (blocks, 8, wide), 0)

    def score_step(c, highest):
        k_copy(c).wait()
        product = jnp.dot(side_by_side(kbuf, c), qdiag[...], preferred_element_type=jnp.float32)
        product = product.reshape(blocks, 8, 2, 8, wide)
        merged = jnp.where(low, product[:, :, 0], product[:, :, 1])
        dense = merged[:, 0]
        for i in range(1, 8):
            dense = jnp.where(turn == i, pltpu.roll(merged[:, i], i, 1), dense)
        dense = jnp.where(base_of(c) < room, dense, masked_fill)
        scores[pl.ds(c * blocks, blocks)] = dense
        return jnp.maximum(highest, jnp.max(dense, axis=0))

    highest = lax.fori_loop(0, n_chunks, score_step, jnp.full((8, wide), masked_fill, jnp.float32))
    highest = jnp.broadcast_to(jnp.max(highest, axis=0, keepdims=True), (8, wide))
    scale = 1.0 / math.sqrt(head_size)

    acc[...] = jnp.zeros_like(acc)
    keep_low = at_home & low
    keep_high = at_home & jnp.logical_not(low)

    def value_step(c, totals):
        v_copy(c).wait()
        dense = scores[pl.ds(c * blocks, blocks)]
        share = jnp.where(base_of(c) < room, jnp.exp((dense - highest) * scale), 0.0)
        spread = []
        for i in range(8):
            turned = pltpu.roll(share, 8 - i, 1) if i else share
            spread.append(
                jnp.concatenate(
                    [jnp.where(keep_low, turned, 0.0), jnp.where(keep_high, turned, 0.0)], axis=1
                ).astype(jnp.bfloat16)
            )
        spread = jnp.stack(spread, axis=1).reshape(STEP * ROWS, wide)
        piece = vbuf[pl.ds(c * STEP, STEP)]
        for g in range(groups):
            acc[g] += lax.dot_general(
                piece[:, g * ROWS:(g + 1) * ROWS].reshape(STEP * ROWS, head_size),
                spread[:, g * lanes:(g + 1) * lanes],
                (((0,), (0,)), ((), ())),
                preferred_element_type=jnp.float32,
            )
        return totals + jnp.sum(share, axis=0)

    totals = lax.fori_loop(0, n_chunks, value_step, jnp.zeros((8, wide), jnp.float32))
    totals = jnp.broadcast_to(jnp.sum(totals, axis=0, keepdims=True), (8, wide))
    for g in range(groups):
        stats[0:head_size, g * lanes:(g + 1) * lanes] = acc[g]
    stats[head_size:head_size + 8] = highest
    stats[head_size + 8:head_size + 16] = totals

    pl.semaphore_wait(barrier, len(greeted))

    sends = []

    def send(source, target, sems, slot, peer):
        copy = pltpu.make_async_remote_copy(
            src_ref=source, dst_ref=target, send_sem=sems.at[0, slot], recv_sem=sems.at[1, slot],
            device_id=peer, device_id_type=MESH,
        )
        copy.start()
        sends.append(copy)
        return copy

    stat_copies = [
        send(stats, got.at[i], stat_sems, i, peer) for i, peer in enumerate(stat_peers)
    ]
    for copy in stat_copies:
        copy.wait_recv()
    tops = [stats[head_size:head_size + 1]] + [
        got[i, head_size:head_size + 1] for i in range(n_split - 1)
    ]
    top = functools.reduce(jnp.maximum, tops)
    total = jnp.zeros((1, wide), jnp.float32)
    summed = jnp.zeros((head_size, wide), jnp.float32)
    for i in range(n_split):
        source = stats if i == 0 else got.at[i - 1]
        factor = jnp.exp((tops[i] - top) * scale)
        total = total + source[head_size + 8:head_size + 9] * factor
        summed = summed + source[0:head_size] * factor
    summed = summed / total
    for g in range(groups):
        flat_att[g] = summed[:, g * lanes:(g + 1) * lanes].T
    start = pl.multiple_of(place * heads_own * ROWS, ROWS)
    attended = jnp.concatenate(
        [
            jnp.concatenate(
                [flat_att[g, pl.ds(start + j * ROWS, ROWS), :] for j in range(heads_own)], axis=1
            )
            for g in range(groups)
        ],
        axis=0,
    ).astype(jnp.bfloat16)

    core_copies, near_copies, far_copies = [], [], []
    for step in range(n_far + 2):
        if step < n_far:
            w_copy(step).wait()
            for n in range(2):
                for s in range(n_seq):
                    at = (n * n_seq + s) * cols
                    part[step, s, n] = jnp.dot(
                        attended, wbuf[step, :, at:at + cols], preferred_element_type=jnp.float32
                    )
            core_copies.append(
                send(part.at[step, other_core], from_core.at[step], core_sems, step, core_peer)
            )
        k = step - 1
        if 0 <= k < n_far:
            core_copies[k].wait_recv()
            pair[k] = part[k, core] + from_core[k]
            near_copies.append(
                send(pair.at[k, 1 - near], from_near.at[k], near_sems, k, near_peer)
            )
        k = step - 2
        if 0 <= k < n_far:
            near_copies[k].wait_recv()
            line[k] = pair[k, near] + from_near[k]
            if offsets[k]:
                far_copies.append(send(line.at[k], from_far.at[k], far_sems, k, far_peers[k]))
    result = line[n_far - 1]
    for k, copy in enumerate(far_copies):
        copy.wait_recv()
        result = result + from_far[k]
    out[...] = result.astype(out.dtype)
    for copy in sends:
        copy.wait_send()


def solution(mesh):
    n_tensor, n_seq = mesh.shape["tensor"], mesh.shape["seq"]

    def body(queries, keys, values, lengths, out_weight):
        span, batch, head_size = keys.shape
        depth, width = out_weight.shape
        per_group = HQ // KVH
        n_flat = n_tensor * n_seq
        cols = width // n_flat
        n_far = n_tensor // 2
        n_split = CACHE // span
        groups = batch // ROWS
        lanes = ROWS * per_group
        wide = groups * lanes
        n_chunks = span // STEP
        q_rows = max(ROWS, per_group)
        f32, bf16 = jnp.float32, jnp.bfloat16
        peers = max(1, n_split - 1)
        return pl.pallas_call(
            functools.partial(kernel, n_tensor, n_seq),
            out_shape=jax.ShapeDtypeStruct((batch, cols), bf16),
            in_specs=[pl.BlockSpec(memory_space=pltpu.SMEM)] + [pl.BlockSpec(memory_space=pl.ANY)] * 4,
            out_specs=pl.BlockSpec(memory_space=pltpu.VMEM),
            scratch_shapes=[
                pltpu.VMEM((span, batch, head_size), bf16),
                pltpu.VMEM((span, batch, head_size), bf16),
                pltpu.VMEM((n_far, depth, 2 * n_seq * cols), bf16),
                pltpu.VMEM((batch, q_rows, head_size), bf16),
                pltpu.VMEM((batch, per_group, head_size), f32),
                pltpu.VMEM((groups * head_size, wide), bf16),
                pltpu.VMEM((span // 8, 8, wide), f32),
                pltpu.VMEM((groups, head_size, lanes), f32),
                pltpu.VMEM((head_size + 16, wide), f32),
                pltpu.VMEM((peers, head_size + 16, wide), f32),
                pltpu.VMEM((groups, lanes, head_size), f32),
                pltpu.VMEM((n_far, n_seq, 2, batch, cols), f32),
                pltpu.VMEM((n_far, 2, batch, cols), f32),
                pltpu.VMEM((n_far, 2, batch, cols), f32),
                pltpu.VMEM((n_far, batch, cols), f32),
                pltpu.VMEM((n_far, batch, cols), f32),
                pltpu.VMEM((n_far, batch, cols), f32),
                pltpu.SemaphoreType.DMA((n_chunks,)),
                pltpu.SemaphoreType.DMA((n_chunks,)),
                pltpu.SemaphoreType.DMA((n_far,)),
                pltpu.SemaphoreType.DMA,
                pltpu.SemaphoreType.DMA((2, peers)),
                pltpu.SemaphoreType.DMA((2, n_far)),
                pltpu.SemaphoreType.DMA((2, n_far)),
                pltpu.SemaphoreType.DMA((2, n_far)),
            ],
            compiler_params=pltpu.CompilerParams(
                collective_id=0, has_side_effects=True, vmem_limit_bytes=60 * 1024 * 1024
            ),
            cost_estimate=pl.CostEstimate(
                flops=4 * span * batch * head_size * per_group + 2 * batch * depth * width,
                bytes_accessed=2 * (2 * span * batch * head_size + depth * width),
                transcendentals=span * batch * per_group,
            ),
        )(lengths, queries, keys, values, out_weight)

    return jax.shard_map(
        body,
        mesh=mesh,
        in_specs=(
            P("groups", None, None),
            P(("tensor", "seq"), "groups", None),
            P(("tensor", "seq"), "groups", None),
            P("groups"),
            P(("tensor", "seq"), None),
        ),
        out_specs=P("groups", ("tensor", "seq")),
        check_vma=False,
    )
```

```python
import functools
import math

import jax
import jax.numpy as jnp
from jax import lax
from jax.experimental import pallas as pl
from jax.experimental.pallas import tpu as pltpu
from jax.sharding import PartitionSpec as P

HQ = 64
KVH = 8
CACHE = 4096

MESH = pl.DeviceIdType.MESH
masked_fill = -1e30
ROWS = 16
STEP = 128


def kernel(
    n_tensor, n_seq, lengths, queries, keys, values, weight, out,
    kbuf, vbuf, wbuf, qbuf, qflat, qdiag, scores, acc, stats, got, flat_att,
    part, from_core, pair, from_near, line, from_far,
    k_sem, v_sem, w_sem, q_sem, stat_sems, core_sems, near_sems, far_sems,
):
    n_flat = n_tensor * n_seq
    span, batch, head_size = keys.shape
    per_group = HQ // KVH
    n_split = CACHE // span
    groups = batch // ROWS
    lanes = ROWS * per_group
    wide = groups * lanes
    depth = groups * head_size
    heads_own = HQ // n_flat
    n_chunks = span // STEP
    cols = out.shape[1]
    n_far = n_tensor // 2
    wide_cols = 2 * n_seq * cols

    group = lax.axis_index("groups")
    tensor = lax.axis_index("tensor")
    core = lax.axis_index("seq")
    flat = tensor * n_seq + core
    kv_head = flat // n_split
    place = flat % n_split
    far, near = tensor // 2, tensor % 2
    other_core = 1 - core

    offsets = sorted(range(n_far), key=lambda off: (-min(off, n_far - off), off))

    def member(index):
        return (group, index // n_seq, index % n_seq)

    stat_peers = [member(kv_head * n_split + (place + k) % n_split) for k in range(1, n_split)]
    core_peer = (group, tensor, other_core)
    near_peer = (group, far * 2 + 1 - near, core)
    far_peers = [(group, (far + off) % n_far * 2 + near, core) for off in offsets]

    barrier = pltpu.get_barrier_semaphore()
    greeted = stat_peers + [core_peer, near_peer] + [
        peer for off, peer in zip(offsets, far_peers) if off
    ]
    for peer in greeted:
        pl.semaphore_signal(barrier, inc=1, device_id=peer, device_id_type=MESH)

    q_rows = ROWS if per_group < ROWS else per_group
    q_start = pl.multiple_of(kv_head * per_group // q_rows * q_rows, q_rows)
    q_copy = pltpu.make_async_copy(queries.at[:, pl.ds(q_start, q_rows), :], qbuf, q_sem)
    q_copy.start()

    def k_copy(c):
        piece = pl.ds(c * STEP, STEP)
        return pltpu.make_async_copy(keys.at[piece], kbuf.at[piece], k_sem.at[c])

    def v_copy(c):
        piece = pl.ds(c * STEP, STEP)
        return pltpu.make_async_copy(values.at[piece], vbuf.at[piece], v_sem.at[c])

    def w_copy(k):
        start = pl.multiple_of((far + offsets[k]) % n_far * wide_cols, wide_cols)
        return pltpu.make_async_copy(weight.at[:, pl.ds(start, wide_cols)], wbuf.at[k], w_sem.at[k])

    @pl.loop(0, n_chunks)
    def _(c):
        k_copy(c).start()

    @pl.loop(0, n_chunks)
    def _(c):
        v_copy(c).start()

    for k in range(n_far):
        w_copy(k).start()

    lane = lax.broadcasted_iota(jnp.int32, (8, wide), 1)
    sub = lax.broadcasted_iota(jnp.int32, (8, wide), 0)
    home = lane % 8
    low = lane % ROWS < 8
    turn = (sub - home + 8) % 8
    at_home = sub == home
    sequence = lane // lanes * ROWS + lane % ROWS
    live_slots = jnp.zeros((8, wide), jnp.int32)
    for b in range(batch):
        live_slots = jnp.where(sequence == b, lengths[b], live_slots)
    first_slot = place * span
    room = live_slots - first_slot - turn

    q_copy.wait()
    q = qbuf[...].astype(jnp.float32)
    if q_rows > per_group:
        q = jnp.where(kv_head % 2 == 0, q[:, :per_group], q[:, per_group:])
    qflat[...] = q
    zero = jnp.zeros((head_size, lanes), jnp.bfloat16)
    for g in range(groups):
        block = jnp.concatenate(
            [qflat[g * ROWS:(g + 1) * ROWS, j, :] for j in range(per_group)], axis=0
        )
        for h in range(groups):
            qdiag[g * head_size:(g + 1) * head_size, h * lanes:(h + 1) * lanes] = (
                block.T.astype(jnp.bfloat16) if g == h else zero
            )

    def side_by_side(buf, c):
        piece = buf[pl.ds(c * STEP, STEP)]
        return jnp.concatenate(
            [
                piece[:, g * ROWS:(g + 1) * ROWS].reshape(STEP * ROWS, head_size)
                for g in range(groups)
            ],
            axis=1,
        )

    blocks = STEP // 8

    def base_of(c):
        return c * STEP + 8 * lax.broadcasted_iota(jnp.int32, (blocks, 8, wide), 0)

    def score_step(c, highest):
        k_copy(c).wait()
        product = jnp.dot(side_by_side(kbuf, c), qdiag[...], preferred_element_type=jnp.float32)
        product = product.reshape(blocks, 8, 2, 8, wide)
        merged = jnp.where(low, product[:, :, 0], product[:, :, 1])
        dense = merged[:, 0]
        for i in range(1, 8):
            dense = jnp.where(turn == i, pltpu.roll(merged[:, i], i, 1), dense)
        dense = jnp.where(base_of(c) < room, dense, masked_fill)
        scores[pl.ds(c * blocks, blocks)] = dense
        return jnp.maximum(highest, jnp.max(dense, axis=0))

    highest = lax.fori_loop(0, n_chunks, score_step, jnp.full((8, wide), masked_fill, jnp.float32))
    highest = jnp.broadcast_to(jnp.max(highest, axis=0, keepdims=True), (8, wide))
    scale = 1.0 / math.sqrt(head_size)

    acc[...] = jnp.zeros_like(acc)
    keep_low = at_home & low
    keep_high = at_home & jnp.logical_not(low)

    def value_step(c, totals):
        v_copy(c).wait()
        dense = scores[pl.ds(c * blocks, blocks)]
        share = jnp.where(base_of(c) < room, jnp.exp((dense - highest) * scale), 0.0)
        spread = []
        for i in range(8):
            turned = pltpu.roll(share, 8 - i, 1) if i else share
            spread.append(
                jnp.concatenate(
                    [jnp.where(keep_low, turned, 0.0), jnp.where(keep_high, turned, 0.0)], axis=1
                ).astype(jnp.bfloat16)
            )
        spread = jnp.stack(spread, axis=1).reshape(STEP * ROWS, wide)
        acc[...] += lax.dot_general(
            side_by_side(vbuf, c), spread, (((0,), (0,)), ((), ())),
            preferred_element_type=jnp.float32,
        )
        return totals + jnp.sum(share, axis=0)

    totals = lax.fori_loop(0, n_chunks, value_step, jnp.zeros((8, wide), jnp.float32))
    totals = jnp.broadcast_to(jnp.sum(totals, axis=0, keepdims=True), (8, wide))
    for g in range(groups):
        stats[0:head_size, g * lanes:(g + 1) * lanes] = acc[
            g * head_size:(g + 1) * head_size, g * lanes:(g + 1) * lanes
        ]
    stats[head_size:head_size + 8] = highest
    stats[head_size + 8:head_size + 16] = totals

    pl.semaphore_wait(barrier, len(greeted))

    sends = []

    def send(source, target, sems, slot, peer):
        copy = pltpu.make_async_remote_copy(
            src_ref=source, dst_ref=target, send_sem=sems.at[0, slot], recv_sem=sems.at[1, slot],
            device_id=peer, device_id_type=MESH,
        )
        copy.start()
        sends.append(copy)
        return copy

    stat_copies = [
        send(stats, got.at[i], stat_sems, i, peer) for i, peer in enumerate(stat_peers)
    ]
    for copy in stat_copies:
        copy.wait_recv()
    tops = [stats[head_size:head_size + 1]] + [
        got[i, head_size:head_size + 1] for i in range(n_split - 1)
    ]
    top = functools.reduce(jnp.maximum, tops)
    total = jnp.zeros((1, wide), jnp.float32)
    summed = jnp.zeros((head_size, wide), jnp.float32)
    for i in range(n_split):
        source = stats if i == 0 else got.at[i - 1]
        factor = jnp.exp((tops[i] - top) * scale)
        total = total + source[head_size + 8:head_size + 9] * factor
        summed = summed + source[0:head_size] * factor
    summed = summed / total
    for g in range(groups):
        flat_att[g] = summed[:, g * lanes:(g + 1) * lanes].T
    start = pl.multiple_of(place * heads_own * ROWS, ROWS)
    attended = jnp.concatenate(
        [
            jnp.concatenate(
                [flat_att[g, pl.ds(start + j * ROWS, ROWS), :] for j in range(heads_own)], axis=1
            )
            for g in range(groups)
        ],
        axis=0,
    ).astype(jnp.bfloat16)

    core_copies, near_copies, far_copies = [], [], []
    for step in range(n_far + 2):
        if step < n_far:
            w_copy(step).wait()
            for n in range(2):
                for s in range(n_seq):
                    at = (n * n_seq + s) * cols
                    part[step, s, n] = jnp.dot(
                        attended, wbuf[step, :, at:at + cols], preferred_element_type=jnp.float32
                    )
            core_copies.append(
                send(part.at[step, other_core], from_core.at[step], core_sems, step, core_peer)
            )
        k = step - 1
        if 0 <= k < n_far:
            core_copies[k].wait_recv()
            pair[k] = part[k, core] + from_core[k]
            near_copies.append(
                send(pair.at[k, 1 - near], from_near.at[k], near_sems, k, near_peer)
            )
        k = step - 2
        if 0 <= k < n_far:
            near_copies[k].wait_recv()
            line[k] = pair[k, near] + from_near[k]
            if offsets[k]:
                far_copies.append(send(line.at[k], from_far.at[k], far_sems, k, far_peers[k]))
    result = line[n_far - 1]
    for k, copy in enumerate(far_copies):
        copy.wait_recv()
        result = result + from_far[k]
    out[...] = result.astype(out.dtype)
    for copy in sends:
        copy.wait_send()


def solution(mesh):
    n_tensor, n_seq = mesh.shape["tensor"], mesh.shape["seq"]

    def body(queries, keys, values, lengths, out_weight):
        span, batch, head_size = keys.shape
        depth, width = out_weight.shape
        per_group = HQ // KVH
        n_flat = n_tensor * n_seq
        cols = width // n_flat
        n_far = n_tensor // 2
        n_split = CACHE // span
        groups = batch // ROWS
        lanes = ROWS * per_group
        wide = groups * lanes
        n_chunks = span // STEP
        q_rows = max(ROWS, per_group)
        f32, bf16 = jnp.float32, jnp.bfloat16
        peers = max(1, n_split - 1)
        return pl.pallas_call(
            functools.partial(kernel, n_tensor, n_seq),
            out_shape=jax.ShapeDtypeStruct((batch, cols), bf16),
            in_specs=[pl.BlockSpec(memory_space=pltpu.SMEM)] + [pl.BlockSpec(memory_space=pl.ANY)] * 4,
            out_specs=pl.BlockSpec(memory_space=pltpu.VMEM),
            scratch_shapes=[
                pltpu.VMEM((span, batch, head_size), bf16),
                pltpu.VMEM((span, batch, head_size), bf16),
                pltpu.VMEM((n_far, depth, 2 * n_seq * cols), bf16),
                pltpu.VMEM((batch, q_rows, head_size), bf16),
                pltpu.VMEM((batch, per_group, head_size), f32),
                pltpu.VMEM((groups * head_size, wide), bf16),
                pltpu.VMEM((span // 8, 8, wide), f32),
                pltpu.VMEM((groups * head_size, wide), f32),
                pltpu.VMEM((head_size + 16, wide), f32),
                pltpu.VMEM((peers, head_size + 16, wide), f32),
                pltpu.VMEM((groups, lanes, head_size), f32),
                pltpu.VMEM((n_far, n_seq, 2, batch, cols), f32),
                pltpu.VMEM((n_far, 2, batch, cols), f32),
                pltpu.VMEM((n_far, 2, batch, cols), f32),
                pltpu.VMEM((n_far, batch, cols), f32),
                pltpu.VMEM((n_far, batch, cols), f32),
                pltpu.VMEM((n_far, batch, cols), f32),
                pltpu.SemaphoreType.DMA((n_chunks,)),
                pltpu.SemaphoreType.DMA((n_chunks,)),
                pltpu.SemaphoreType.DMA((n_far,)),
                pltpu.SemaphoreType.DMA,
                pltpu.SemaphoreType.DMA((2, peers)),
                pltpu.SemaphoreType.DMA((2, n_far)),
                pltpu.SemaphoreType.DMA((2, n_far)),
                pltpu.SemaphoreType.DMA((2, n_far)),
            ],
            compiler_params=pltpu.CompilerParams(
                collective_id=0, has_side_effects=True, vmem_limit_bytes=60 * 1024 * 1024
            ),
            cost_estimate=pl.CostEstimate(
                flops=4 * span * batch * head_size * per_group + 2 * batch * depth * width,
                bytes_accessed=2 * (2 * span * batch * head_size + depth * width),
                transcendentals=span * batch * per_group,
            ),
        )(lengths, queries, keys, values, out_weight)

    return jax.shard_map(
        body,
        mesh=mesh,
        in_specs=(
            P("groups", None, None),
            P(("tensor", "seq"), "groups", None),
            P(("tensor", "seq"), "groups", None),
            P("groups"),
            P(("tensor", "seq"), None),
        ),
        out_specs=P("groups", ("tensor", "seq")),
        check_vma=False,
    )
```

```python
import functools
import math

import jax
import jax.numpy as jnp
from jax import lax
from jax.experimental import pallas as pl
from jax.experimental.pallas import tpu as pltpu
from jax.sharding import PartitionSpec as P

HQ = 64
KVH = 8
CACHE = 4096

MESH = pl.DeviceIdType.MESH
masked_fill = -1e30
ROWS = 16
STEP = 128
SIDES = 2


def kernel(
    n_tensor, n_seq, lengths, queries, keys, values, weight, out,
    kbuf, vbuf, wbuf, qbuf, qflat, qdiag, scores, acc, stats, got, flat_att,
    part, from_core, pair, from_near, line, from_far,
    k_sem, v_sem, w_sem, q_sem, stat_sems, core_sems, near_sems, far_sems,
):
    n_flat = n_tensor * n_seq
    span, batch, head_size = keys.shape
    per_group = HQ // KVH
    n_split = CACHE // span
    groups = batch // ROWS
    lanes = ROWS * per_group
    wide = SIDES * lanes
    reach = span // SIDES
    heads_own = HQ // n_flat
    n_chunks = reach // STEP
    cols = out.shape[1]
    n_far = n_tensor // 2
    wide_cols = 2 * n_seq * cols
    scale = 1.0 / math.sqrt(head_size)

    group = lax.axis_index("groups")
    tensor = lax.axis_index("tensor")
    core = lax.axis_index("seq")
    flat = tensor * n_seq + core
    kv_head = flat // n_split
    place = flat % n_split
    far, near = tensor // 2, tensor % 2
    other_core = 1 - core

    offsets = sorted(range(n_far), key=lambda off: (-min(off, n_far - off), off))

    def member(index):
        return (group, index // n_seq, index % n_seq)

    stat_peers = [member(kv_head * n_split + (place + k) % n_split) for k in range(1, n_split)]
    core_peer = (group, tensor, other_core)
    near_peer = (group, far * 2 + 1 - near, core)
    far_peers = [(group, (far + off) % n_far * 2 + near, core) for off in offsets]

    barrier = pltpu.get_barrier_semaphore()
    greeted = stat_peers + [core_peer, near_peer] + [
        peer for off, peer in zip(offsets, far_peers) if off
    ]
    for peer in greeted:
        pl.semaphore_signal(barrier, inc=1, device_id=peer, device_id_type=MESH)

    q_rows = ROWS if per_group < ROWS else per_group
    q_start = pl.multiple_of(kv_head * per_group // q_rows * q_rows, q_rows)
    q_copy = pltpu.make_async_copy(queries.at[:, pl.ds(q_start, q_rows), :], qbuf, q_sem)
    q_copy.start()

    def cache_copy(cache, buf, sems, g, side, c):
        piece = pl.ds(side * reach + c * STEP, STEP)
        return pltpu.make_async_copy(
            cache.at[piece, g * ROWS:(g + 1) * ROWS], buf.at[g, piece], sems.at[g, side, c]
        )

    def start_cache(cache, buf, sems, g):
        @pl.loop(0, n_chunks)
        def _(c):
            for side in range(SIDES):
                cache_copy(cache, buf, sems, g, side, c).start()

    def w_copy(k):
        start = pl.multiple_of((far + offsets[k]) % n_far * wide_cols, wide_cols)
        return pltpu.make_async_copy(weight.at[:, pl.ds(start, wide_cols)], wbuf.at[k], w_sem.at[k])

    for g in range(groups):
        start_cache(keys, kbuf, k_sem, g)
        if g == groups - 1:
            for k in range(n_far):
                w_copy(k).start()
        start_cache(values, vbuf, v_sem, g)

    lane = lax.broadcasted_iota(jnp.int32, (8, wide), 1)
    sub = lax.broadcasted_iota(jnp.int32, (8, wide), 0)
    home = lane % 8
    low = lane % ROWS < 8
    turn = (sub - home + 8) % 8
    at_home = sub == home
    keep_low = at_home & low
    keep_high = at_home & jnp.logical_not(low)
    taken = place * span + lane // lanes * reach + turn

    def room_of(g):
        live_slots = jnp.zeros((8, wide), jnp.int32)
        for b in range(ROWS):
            live_slots = jnp.where(lane % ROWS == b, lengths[g * ROWS + b], live_slots)
        return live_slots - taken

    q_copy.wait()
    q = qbuf[...].astype(jnp.float32)
    if q_rows > per_group:
        q = jnp.where(kv_head % 2 == 0, q[:, :per_group], q[:, per_group:])
    qflat[...] = q
    qdiag[...] = jnp.zeros_like(qdiag)
    for g in range(groups):
        block = jnp.concatenate(
            [qflat[g * ROWS:(g + 1) * ROWS, j, :] for j in range(per_group)], axis=0
        ).T.astype(jnp.bfloat16)
        for side in range(SIDES):
            qdiag[
                g, side * head_size:(side + 1) * head_size, side * lanes:(side + 1) * lanes
            ] = block

    def side_by_side(buf, g, c):
        return jnp.concatenate(
            [
                buf[g, pl.ds(side * reach + c * STEP, STEP)].reshape(STEP * ROWS, head_size)
                for side in range(SIDES)
            ],
            axis=1,
        )

    blocks = STEP // 8

    def base_of(c):
        return c * STEP + 8 * lax.broadcasted_iota(jnp.int32, (blocks, 8, wide), 0)

    def both_sides(row, merge):
        return functools.reduce(
            merge, [row[:, side * lanes:(side + 1) * lanes] for side in range(SIDES)]
        )

    def score_pass(g, room):
        def step(c, highest):
            for side in range(SIDES):
                cache_copy(keys, kbuf, k_sem, g, side, c).wait()
            product = jnp.dot(
                side_by_side(kbuf, g, c), qdiag[g], preferred_element_type=jnp.float32
            ).reshape(blocks, 8, 2, 8, wide)
            merged = jnp.where(low, product[:, :, 0], product[:, :, 1])
            dense = merged[:, 0]
            for i in range(1, 8):
                dense = jnp.where(turn == i, pltpu.roll(merged[:, i], i, 1), dense)
            dense = jnp.where(base_of(c) < room, dense, masked_fill)
            scores[pl.ds(c * blocks, blocks)] = dense
            return jnp.maximum(highest, jnp.max(dense, axis=0))

        highest = lax.fori_loop(0, n_chunks, step, jnp.full((8, wide), masked_fill, jnp.float32))
        return both_sides(jnp.max(highest, axis=0, keepdims=True), jnp.maximum)

    def value_pass(g, room, highest, first, last, totals):
        level = jnp.broadcast_to(jnp.concatenate([highest] * SIDES, axis=1), (8, wide))

        def step(c, totals):
            for side in range(SIDES):
                cache_copy(values, vbuf, v_sem, g, side, c).wait()
            dense = scores[pl.ds(c * blocks, blocks)]
            share = jnp.where(base_of(c) < room, jnp.exp((dense - level) * scale), 0.0)
            spread = []
            for i in range(8):
                turned = pltpu.roll(share, 8 - i, 1) if i else share
                spread.append(
                    jnp.concatenate(
                        [jnp.where(keep_low, turned, 0.0), jnp.where(keep_high, turned, 0.0)],
                        axis=1,
                    ).astype(jnp.bfloat16)
                )
            spread = jnp.stack(spread, axis=1).reshape(STEP * ROWS, wide)
            acc[...] += lax.dot_general(
                side_by_side(vbuf, g, c), spread, (((0,), (0,)), ((), ())),
                preferred_element_type=jnp.float32,
            )
            return totals + jnp.sum(share, axis=0)

        return lax.fori_loop(first, last, step, totals)

    sends = []

    def send(source, target, sems, slot, peer):
        copy = pltpu.make_async_remote_copy(
            src_ref=source, dst_ref=target,
            send_sem=sems.at[(0,) + slot], recv_sem=sems.at[(1,) + slot],
            device_id=peer, device_id_type=MESH,
        )
        copy.start()
        sends.append(copy)
        return copy

    def send_stats(g, highest, totals):
        stats[g, 0:head_size] = functools.reduce(
            jnp.add,
            [
                acc[side * head_size:(side + 1) * head_size, side * lanes:(side + 1) * lanes]
                for side in range(SIDES)
            ],
        )
        total = both_sides(jnp.sum(totals, axis=0, keepdims=True), jnp.add)
        stats[g, head_size:head_size + 8] = jnp.broadcast_to(highest, (8, lanes))
        stats[g, head_size + 8:head_size + 16] = jnp.broadcast_to(total, (8, lanes))
        return [
            send(stats.at[g], got.at[g, i], stat_sems, (g, i), peer)
            for i, peer in enumerate(stat_peers)
        ]

    def attended_of(g, copies):
        for copy in copies:
            copy.wait_recv()
        sources = [stats.at[g]] + [got.at[g, i] for i in range(n_split - 1)]
        tops = [source[head_size:head_size + 1] for source in sources]
        top = functools.reduce(jnp.maximum, tops)
        total = jnp.zeros((1, lanes), jnp.float32)
        summed = jnp.zeros((head_size, lanes), jnp.float32)
        for source, own_top in zip(sources, tops):
            factor = jnp.exp((own_top - top) * scale)
            total = total + source[head_size + 8:head_size + 9] * factor
            summed = summed + source[0:head_size] * factor
        flat_att[g] = (summed / total).T
        start = pl.multiple_of(place * heads_own * ROWS, ROWS)
        return jnp.concatenate(
            [flat_att[g, pl.ds(start + j * ROWS, ROWS), :] for j in range(heads_own)], axis=1
        ).astype(jnp.bfloat16)

    core_copies, near_copies, far_copies = {}, {}, {}

    def project(g, attended, k):
        if g == 0:
            w_copy(k).wait()
        for n in range(2):
            for s in range(n_seq):
                at = (n * n_seq + s) * cols
                part[g, k, s, n] = jnp.dot(
                    attended, wbuf[k, :, at:at + cols], preferred_element_type=jnp.float32
                )
        core_copies[g, k] = send(
            part.at[g, k, other_core], from_core.at[g, k], core_sems, (g, k), core_peer
        )

    def to_near(g, k):
        core_copies[g, k].wait_recv()
        pair[g, k] = part[g, k, core] + from_core[g, k]
        near_copies[g, k] = send(
            pair.at[g, k, 1 - near], from_near.at[g, k], near_sems, (g, k), near_peer
        )

    def to_far(g, k):
        near_copies[g, k].wait_recv()
        line[g, k] = pair[g, k, near] + from_near[g, k]
        if offsets[k]:
            far_copies[g, k] = send(
                line.at[g, k], from_far.at[g, k], far_sems, (g, k), far_peers[k]
            )

    waiting = None
    for g in range(groups):
        room = room_of(g)
        highest = score_pass(g, room)
        if g:
            attended = attended_of(g - 1, waiting)
            for k in range(n_far):
                project(g - 1, attended, k)
        acc[...] = jnp.zeros_like(acc)
        totals = jnp.zeros((8, wide), jnp.float32)
        if g:
            cuts = [0, n_chunks // 4, n_chunks * 3 // 4, n_chunks]
            totals = value_pass(g, room, highest, cuts[0], cuts[1], totals)
            for k in range(n_far):
                to_near(g - 1, k)
            totals = value_pass(g, room, highest, cuts[1], cuts[2], totals)
            for k in range(n_far):
                to_far(g - 1, k)
            totals = value_pass(g, room, highest, cuts[2], cuts[3], totals)
        else:
            totals = value_pass(g, room, highest, 0, n_chunks, totals)
            pl.semaphore_wait(barrier, len(greeted))
        waiting = send_stats(g, highest, totals)

    g = groups - 1
    attended = attended_of(g, waiting)
    for step in range(n_far + 2):
        if step < n_far:
            project(g, attended, step)
        if 0 <= step - 1 < n_far:
            to_near(g, step - 1)
        if 0 <= step - 2 < n_far:
            to_far(g, step - 2)
    for g in range(groups):
        result = line[g, n_far - 1]
        for k in range(n_far - 1):
            far_copies[g, k].wait_recv()
            result = result + from_far[g, k]
        out[g * ROWS:(g + 1) * ROWS] = result.astype(out.dtype)
    for copy in sends:
        copy.wait_send()


def solution(mesh):
    n_tensor, n_seq = mesh.shape["tensor"], mesh.shape["seq"]

    def body(queries, keys, values, lengths, out_weight):
        span, batch, head_size = keys.shape
        depth, width = out_weight.shape
        per_group = HQ // KVH
        n_flat = n_tensor * n_seq
        cols = width // n_flat
        n_far = n_tensor // 2
        n_split = CACHE // span
        groups = batch // ROWS
        lanes = ROWS * per_group
        wide = SIDES * lanes
        n_chunks = span // SIDES // STEP
        q_rows = max(ROWS, per_group)
        f32, bf16 = jnp.float32, jnp.bfloat16
        peers = max(1, n_split - 1)
        return pl.pallas_call(
            functools.partial(kernel, n_tensor, n_seq),
            out_shape=jax.ShapeDtypeStruct((batch, cols), bf16),
            in_specs=[pl.BlockSpec(memory_space=pltpu.SMEM)] + [pl.BlockSpec(memory_space=pl.ANY)] * 4,
            out_specs=pl.BlockSpec(memory_space=pltpu.VMEM),
            scratch_shapes=[
                pltpu.VMEM((groups, span, ROWS, head_size), bf16),
                pltpu.VMEM((groups, span, ROWS, head_size), bf16),
                pltpu.VMEM((n_far, depth, 2 * n_seq * cols), bf16),
                pltpu.VMEM((batch, q_rows, head_size), bf16),
                pltpu.VMEM((batch, per_group, head_size), f32),
                pltpu.VMEM((groups, SIDES * head_size, wide), bf16),
                pltpu.VMEM((span // SIDES // 8, 8, wide), f32),
                pltpu.VMEM((SIDES * head_size, wide), f32),
                pltpu.VMEM((groups, head_size + 16, lanes), f32),
                pltpu.VMEM((groups, peers, head_size + 16, lanes), f32),
                pltpu.VMEM((groups, lanes, head_size), f32),
                pltpu.VMEM((groups, n_far, n_seq, 2, ROWS, cols), f32),
                pltpu.VMEM((groups, n_far, 2, ROWS, cols), f32),
                pltpu.VMEM((groups, n_far, 2, ROWS, cols), f32),
                pltpu.VMEM((groups, n_far, ROWS, cols), f32),
                pltpu.VMEM((groups, n_far, ROWS, cols), f32),
                pltpu.VMEM((groups, n_far, ROWS, cols), f32),
                pltpu.SemaphoreType.DMA((groups, SIDES, n_chunks)),
                pltpu.SemaphoreType.DMA((groups, SIDES, n_chunks)),
                pltpu.SemaphoreType.DMA((n_far,)),
                pltpu.SemaphoreType.DMA,
                pltpu.SemaphoreType.DMA((2, groups, peers)),
                pltpu.SemaphoreType.DMA((2, groups, n_far)),
                pltpu.SemaphoreType.DMA((2, groups, n_far)),
                pltpu.SemaphoreType.DMA((2, groups, n_far)),
            ],
            compiler_params=pltpu.CompilerParams(
                collective_id=0, has_side_effects=True, vmem_limit_bytes=60 * 1024 * 1024
            ),
            cost_estimate=pl.CostEstimate(
                flops=4 * span * batch * head_size * per_group + 2 * batch * depth * width,
                bytes_accessed=2 * (2 * span * batch * head_size + depth * width),
                transcendentals=span * batch * per_group,
            ),
        )(lengths, queries, keys, values, out_weight)

    return jax.shard_map(
        body,
        mesh=mesh,
        in_specs=(
            P("groups", None, None),
            P(("tensor", "seq"), "groups", None),
            P(("tensor", "seq"), "groups", None),
            P("groups"),
            P(("tensor", "seq"), None),
        ),
        out_specs=P("groups", ("tensor", "seq")),
        check_vma=False,
    )
```

```python
import functools
import math

import jax
import jax.numpy as jnp
from jax import lax
from jax.experimental import pallas as pl
from jax.experimental.pallas import tpu as pltpu
from jax.sharding import PartitionSpec as P

HQ = 64
KVH = 8
CACHE = 4096

MESH = pl.DeviceIdType.MESH
masked_fill = -1e30
ROWS = 16
STEP = 256


def kernel(
    n_tensor, n_seq, lengths, queries, keys, values, weight, out,
    kbuf, vbuf, wbuf, qbuf, qflat, qdiag, scores, acc, stats, got, flat_att,
    part, from_core, pair, from_near, line, from_far,
    k_sem, v_sem, w_sem, q_sem, stat_sems, core_sems, near_sems, far_sems,
):
    n_flat = n_tensor * n_seq
    span, batch, head_size = keys.shape
    per_group = HQ // KVH
    n_split = CACHE // span
    groups = batch // ROWS
    lanes = ROWS * per_group
    wide = groups * lanes
    depth = groups * head_size
    heads_own = HQ // n_flat
    n_chunks = span // STEP
    cols = out.shape[1]
    n_far = n_tensor // 2
    wide_cols = 2 * n_seq * cols

    group = lax.axis_index("groups")
    tensor = lax.axis_index("tensor")
    core = lax.axis_index("seq")
    flat = tensor * n_seq + core
    kv_head = flat // n_split
    place = flat % n_split
    far, near = tensor // 2, tensor % 2
    other_core = 1 - core

    offsets = sorted(range(n_far), key=lambda off: (-min(off, n_far - off), off))

    def member(index):
        return (group, index // n_seq, index % n_seq)

    stat_peers = [member(kv_head * n_split + (place + k) % n_split) for k in range(1, n_split)]
    core_peer = (group, tensor, other_core)
    near_peer = (group, far * 2 + 1 - near, core)
    far_peers = [(group, (far + off) % n_far * 2 + near, core) for off in offsets]

    barrier = pltpu.get_barrier_semaphore()
    greeted = stat_peers + [core_peer, near_peer] + [
        peer for off, peer in zip(offsets, far_peers) if off
    ]
    for peer in greeted:
        pl.semaphore_signal(barrier, inc=1, device_id=peer, device_id_type=MESH)

    q_rows = ROWS if per_group < ROWS else per_group
    q_start = pl.multiple_of(kv_head * per_group // q_rows * q_rows, q_rows)
    q_copy = pltpu.make_async_copy(queries.at[:, pl.ds(q_start, q_rows), :], qbuf, q_sem)
    q_copy.start()

    def k_copy(c):
        piece = pl.ds(c * STEP, STEP)
        return pltpu.make_async_copy(keys.at[piece], kbuf.at[piece], k_sem.at[c])

    def v_copy(c):
        piece = pl.ds(c * STEP, STEP)
        return pltpu.make_async_copy(values.at[piece], vbuf.at[piece], v_sem.at[c])

    def w_copy(k):
        start = pl.multiple_of((far + offsets[k]) % n_far * wide_cols, wide_cols)
        return pltpu.make_async_copy(weight.at[:, pl.ds(start, wide_cols)], wbuf.at[k], w_sem.at[k])

    @pl.loop(0, n_chunks)
    def _(c):
        k_copy(c).start()

    @pl.loop(0, n_chunks)
    def _(c):
        v_copy(c).start()

    for k in range(n_far):
        w_copy(k).start()

    lane = lax.broadcasted_iota(jnp.int32, (8, wide), 1)
    sub = lax.broadcasted_iota(jnp.int32, (8, wide), 0)
    home = lane % 8
    low = lane % ROWS < 8
    turn = (sub - home + 8) % 8
    at_home = sub == home
    sequence = lane // lanes * ROWS + lane % ROWS
    live_slots = jnp.zeros((8, wide), jnp.int32)
    for b in range(batch):
        live_slots = jnp.where(sequence == b, lengths[b], live_slots)
    first_slot = place * span
    room = live_slots - first_slot - turn

    q_copy.wait()
    q = qbuf[...].astype(jnp.float32)
    if q_rows > per_group:
        q = jnp.where(kv_head % 2 == 0, q[:, :per_group], q[:, per_group:])
    qflat[...] = q
    zero = jnp.zeros((head_size, lanes), jnp.bfloat16)
    for g in range(groups):
        block = jnp.concatenate(
            [qflat[g * ROWS:(g + 1) * ROWS, j, :] for j in range(per_group)], axis=0
        )
        for h in range(groups):
            qdiag[g * head_size:(g + 1) * head_size, h * lanes:(h + 1) * lanes] = (
                block.T.astype(jnp.bfloat16) if g == h else zero
            )

    def side_by_side(buf, c):
        piece = buf[pl.ds(c * STEP, STEP)]
        return jnp.concatenate(
            [
                piece[:, g * ROWS:(g + 1) * ROWS].reshape(STEP * ROWS, head_size)
                for g in range(groups)
            ],
            axis=1,
        )

    blocks = STEP // 8

    def base_of(c):
        return c * STEP + 8 * lax.broadcasted_iota(jnp.int32, (blocks, 8, wide), 0)

    def score_step(c, highest):
        k_copy(c).wait()
        product = jnp.dot(side_by_side(kbuf, c), qdiag[...], preferred_element_type=jnp.float32)
        product = product.reshape(blocks, 8, 2, 8, wide)
        merged = jnp.where(low, product[:, :, 0], product[:, :, 1])
        dense = merged[:, 0]
        for i in range(1, 8):
            dense = jnp.where(turn == i, pltpu.roll(merged[:, i], i, 1), dense)
        dense = jnp.where(base_of(c) < room, dense, masked_fill)
        scores[pl.ds(c * blocks, blocks)] = dense
        return jnp.maximum(highest, jnp.max(dense, axis=0))

    highest = lax.fori_loop(0, n_chunks, score_step, jnp.full((8, wide), masked_fill, jnp.float32))
    highest = jnp.broadcast_to(jnp.max(highest, axis=0, keepdims=True), (8, wide))
    scale = 1.0 / math.sqrt(head_size)

    acc[...] = jnp.zeros_like(acc)
    keep = jnp.concatenate(
        [
            jnp.where(at_home & low, 1.0, 0.0),
            jnp.where(at_home & jnp.logical_not(low), 1.0, 0.0),
        ],
        axis=0,
    ).astype(jnp.bfloat16)

    def value_step(c, totals):
        v_copy(c).wait()
        dense = scores[pl.ds(c * blocks, blocks)]
        share = jnp.where(base_of(c) < room, jnp.exp((dense - highest) * scale), 0.0)
        spread = []
        for i in range(8):
            turned = pltpu.roll(share, 8 - i, 1) if i else share
            spread.append(
                jnp.concatenate([turned, turned], axis=1).astype(jnp.bfloat16) * keep
            )
        spread = jnp.stack(spread, axis=1).reshape(STEP * ROWS, wide)
        acc[...] += lax.dot_general(
            side_by_side(vbuf, c), spread, (((0,), (0,)), ((), ())),
            preferred_element_type=jnp.float32,
        )
        return totals + jnp.sum(share, axis=0)

    totals = lax.fori_loop(0, n_chunks, value_step, jnp.zeros((8, wide), jnp.float32))
    totals = jnp.broadcast_to(jnp.sum(totals, axis=0, keepdims=True), (8, wide))
    for g in range(groups):
        stats[0:head_size, g * lanes:(g + 1) * lanes] = acc[
            g * head_size:(g + 1) * head_size, g * lanes:(g + 1) * lanes
        ]
    stats[head_size:head_size + 8] = highest
    stats[head_size + 8:head_size + 16] = totals

    pl.semaphore_wait(barrier, len(greeted))

    sends = []

    def send(source, target, sems, slot, peer):
        copy = pltpu.make_async_remote_copy(
            src_ref=source, dst_ref=target, send_sem=sems.at[0, slot], recv_sem=sems.at[1, slot],
            device_id=peer, device_id_type=MESH,
        )
        copy.start()
        sends.append(copy)
        return copy

    stat_copies = [
        send(stats, got.at[i], stat_sems, i, peer) for i, peer in enumerate(stat_peers)
    ]
    for copy in stat_copies:
        copy.wait_recv()
    tops = [stats[head_size:head_size + 1]] + [
        got[i, head_size:head_size + 1] for i in range(n_split - 1)
    ]
    top = functools.reduce(jnp.maximum, tops)
    total = jnp.zeros((1, wide), jnp.float32)
    summed = jnp.zeros((head_size, wide), jnp.float32)
    for i in range(n_split):
        source = stats if i == 0 else got.at[i - 1]
        factor = jnp.exp((tops[i] - top) * scale)
        total = total + source[head_size + 8:head_size + 9] * factor
        summed = summed + source[0:head_size] * factor
    summed = summed / total
    for g in range(groups):
        flat_att[g] = summed[:, g * lanes:(g + 1) * lanes].T
    start = pl.multiple_of(place * heads_own * ROWS, ROWS)
    attended = jnp.concatenate(
        [
            jnp.concatenate(
                [flat_att[g, pl.ds(start + j * ROWS, ROWS), :] for j in range(heads_own)], axis=1
            )
            for g in range(groups)
        ],
        axis=0,
    ).astype(jnp.bfloat16)

    core_copies, near_copies, far_copies = [], [], []
    for step in range(n_far + 2):
        if step < n_far:
            w_copy(step).wait()
            for n in range(2):
                for s in range(n_seq):
                    at = (n * n_seq + s) * cols
                    part[step, s, n] = jnp.dot(
                        attended, wbuf[step, :, at:at + cols], preferred_element_type=jnp.float32
                    )
            core_copies.append(
                send(part.at[step, other_core], from_core.at[step], core_sems, step, core_peer)
            )
        k = step - 1
        if 0 <= k < n_far:
            core_copies[k].wait_recv()
            pair[k] = part[k, core] + from_core[k]
            near_copies.append(
                send(pair.at[k, 1 - near], from_near.at[k], near_sems, k, near_peer)
            )
        k = step - 2
        if 0 <= k < n_far:
            near_copies[k].wait_recv()
            line[k] = pair[k, near] + from_near[k]
            if offsets[k]:
                far_copies.append(send(line.at[k], from_far.at[k], far_sems, k, far_peers[k]))
    result = line[n_far - 1]
    for k, copy in enumerate(far_copies):
        copy.wait_recv()
        result = result + from_far[k]
    out[...] = result.astype(out.dtype)
    for copy in sends:
        copy.wait_send()


def solution(mesh):
    n_tensor, n_seq = mesh.shape["tensor"], mesh.shape["seq"]

    def body(queries, keys, values, lengths, out_weight):
        span, batch, head_size = keys.shape
        depth, width = out_weight.shape
        per_group = HQ // KVH
        n_flat = n_tensor * n_seq
        cols = width // n_flat
        n_far = n_tensor // 2
        n_split = CACHE // span
        groups = batch // ROWS
        lanes = ROWS * per_group
        wide = groups * lanes
        n_chunks = span // STEP
        q_rows = max(ROWS, per_group)
        f32, bf16 = jnp.float32, jnp.bfloat16
        peers = max(1, n_split - 1)
        return pl.pallas_call(
            functools.partial(kernel, n_tensor, n_seq),
            out_shape=jax.ShapeDtypeStruct((batch, cols), bf16),
            in_specs=[pl.BlockSpec(memory_space=pltpu.SMEM)] + [pl.BlockSpec(memory_space=pl.ANY)] * 4,
            out_specs=pl.BlockSpec(memory_space=pltpu.VMEM),
            scratch_shapes=[
                pltpu.VMEM((span, batch, head_size), bf16),
                pltpu.VMEM((span, batch, head_size), bf16),
                pltpu.VMEM((n_far, depth, 2 * n_seq * cols), bf16),
                pltpu.VMEM((batch, q_rows, head_size), bf16),
                pltpu.VMEM((batch, per_group, head_size), f32),
                pltpu.VMEM((groups * head_size, wide), bf16),
                pltpu.VMEM((span // 8, 8, wide), f32),
                pltpu.VMEM((groups * head_size, wide), f32),
                pltpu.VMEM((head_size + 16, wide), f32),
                pltpu.VMEM((peers, head_size + 16, wide), f32),
                pltpu.VMEM((groups, lanes, head_size), f32),
                pltpu.VMEM((n_far, n_seq, 2, batch, cols), f32),
                pltpu.VMEM((n_far, 2, batch, cols), f32),
                pltpu.VMEM((n_far, 2, batch, cols), f32),
                pltpu.VMEM((n_far, batch, cols), f32),
                pltpu.VMEM((n_far, batch, cols), f32),
                pltpu.VMEM((n_far, batch, cols), f32),
                pltpu.SemaphoreType.DMA((n_chunks,)),
                pltpu.SemaphoreType.DMA((n_chunks,)),
                pltpu.SemaphoreType.DMA((n_far,)),
                pltpu.SemaphoreType.DMA,
                pltpu.SemaphoreType.DMA((2, peers)),
                pltpu.SemaphoreType.DMA((2, n_far)),
                pltpu.SemaphoreType.DMA((2, n_far)),
                pltpu.SemaphoreType.DMA((2, n_far)),
            ],
            compiler_params=pltpu.CompilerParams(
                collective_id=0, has_side_effects=True, vmem_limit_bytes=60 * 1024 * 1024
            ),
            cost_estimate=pl.CostEstimate(
                flops=4 * span * batch * head_size * per_group + 2 * batch * depth * width,
                bytes_accessed=2 * (2 * span * batch * head_size + depth * width),
                transcendentals=span * batch * per_group,
            ),
        )(lengths, queries, keys, values, out_weight)

    return jax.shard_map(
        body,
        mesh=mesh,
        in_specs=(
            P("groups", None, None),
            P(("tensor", "seq"), "groups", None),
            P(("tensor", "seq"), "groups", None),
            P("groups"),
            P(("tensor", "seq"), None),
        ),
        out_specs=P("groups", ("tensor", "seq")),
        check_vma=False,
    )
```
